32 devices in a mesh: row: 4 (over z), col: 2 (over x), rep: 4 (over y, core).
Axes of the slice: x: 2, y: 2, z: 4, core: 2. Of those that a mesh axis runs over, the one named last changes fastest.
Arguments:
- density: float32 [1024, 1024], P(('col', 'rep'), 'row'), may hold values from -0.25 to 1.25, as said below
- pattern: int32 [16, 9], replicated, may hold values from 0 to 15, as said below
- grid_order: int32 [16], replicated, may hold values from 0 to 15, as said below
Outputs:
- purified: float32 [1024, 1024], P(('col', 'rep'), 'row')
The draws below stay inside these ranges and needn't reach their ends.
Inputs may be any that keep to these rules, and one draw needn't show every extreme that they name: `pattern`: row r lists (r + d) mod 16 for one set of 9 distinct offsets d that holds 0 and is closed under negation modulo 16. `grid_order`: each block index appears once. `density`: Symmetric; zero outside the blocks that the pattern lists.
All inputs are finite; a program needn't handle non-finite values.
Results may differ from the reference program's by a relative error of at most 0.00016.
Values sent between devices are 32-bit elements; how exact they have to be, the bound alone decides.
No kernel may reach another device: no remote copies, remote signals or barrier semaphores. Data moves between devices by JAX's collectives and lax.ppermute only.
A program may use at most 64 MiB of HBM per device.

```python
import math
import jax
import jax.numpy as jnp
from jax import lax

BLOCK = 64
ROW_NONZERO = 9
STEPS = 2
BLOCKS = 16


def pattern_parts(key):
    order = jax.random.permutation(jax.random.fold_in(key, 11), BLOCKS).astype(jnp.int32)
    chosen = jax.random.permutation(jax.random.fold_in(key, 12), BLOCKS // 2 - 1)[:(ROW_NONZERO - 1) // 2].astype(jnp.int32) + 1
    offsets = jnp.concatenate([jnp.zeros((1,), jnp.int32), chosen, BLOCKS - chosen]).astype(jnp.int32)
    return (order, offsets)


def draw_pattern(key, part):
    order, offsets = pattern_parts(key)
    every = jnp.arange(BLOCKS, dtype=jnp.int32)
    return ((every[:, None] + offsets[None, :]) % BLOCKS).astype(jnp.int32)


def draw_grid_order(key, part):
    order, offsets = pattern_parts(key)
    return order


def draw_density(key, part):
    order, offsets = pattern_parts(key)
    width = BLOCK * BLOCKS
    spread = 0.25 / math.sqrt(BLOCK * ROW_NONZERO)
    noise = jax.random.truncated_normal(jax.random.fold_in(key, 21), -4.0, 4.0, (width, width), jnp.float32)
    diagonal = jax.random.uniform(jax.random.fold_in(key, 22), (width,), jnp.float32, 0.1, 0.9)
    symmetric = (noise + noise.T) * (spread / math.sqrt(2.0))
    every = jnp.arange(BLOCKS, dtype=jnp.int32)
    distance = (every[None, :] - every[:, None]) % BLOCKS
    nearby = jnp.any(distance[:, :, None] == offsets[None, None, :], axis=2).astype(jnp.float32)
    nearby_cells = jnp.repeat(jnp.repeat(nearby, BLOCK, axis=0), BLOCK, axis=1)
    natural = nearby_cells * symmetric + jnp.diag(diagonal)
    cells = (order[:, None] * BLOCK + jnp.arange(BLOCK, dtype=jnp.int32)[None, :]).reshape(-1)
    return natural[cells][:, cells]


def setup_inputs(seed: int = 0) -> dict:
    key_of = jax.random.split(jax.random.key(seed), 4)
    density = draw_density(jax.random.fold_in(key_of[3], 71), 0)
    pattern = draw_pattern(jax.random.fold_in(key_of[3], 71), 0)
    grid_order = draw_grid_order(jax.random.fold_in(key_of[3], 71), 0)
    return {"density": density, "pattern": pattern, "grid_order": grid_order}


def reference(density, pattern, grid_order):
    listed = pattern[grid_order]
    hits = jnp.any(listed[:, :, None] == grid_order[None, None, :], axis=1)
    mask = jnp.repeat(jnp.repeat(hits.astype(jnp.float32), BLOCK, axis=0), BLOCK, axis=1)
    current = density
    for repeat in range(STEPS):
        square = jnp.dot(current, current, precision=lax.Precision.HIGHEST, preferred_element_type=jnp.float32)
        cube = jnp.dot(square, current, precision=lax.Precision.HIGHEST, preferred_element_type=jnp.float32)
        current = mask * (3.0 * square - 2.0 * cube)
    return current
```

```python
import functools

import jax
import jax.numpy as jnp
from jax import lax
from jax.experimental import pallas as pl
from jax.experimental.pallas import tpu as pltpu
from jax.sharding import PartitionSpec as P

STEPS = 2
AXES = ("row", "col", "rep")
VMEM_BYTES = 52 * 2**20
EXTRA = 8


def block_mask(pattern, grid_order, first_row, first_col, row_blocks, col_blocks):
    total = grid_order.shape[0]
    every = jnp.arange(total, dtype=jnp.int32)
    row_ids = first_row + jnp.arange(row_blocks, dtype=jnp.int32)
    col_ids = first_col + jnp.arange(col_blocks, dtype=jnp.int32)
    row_pick = (row_ids[:, None] == every[None, :]).astype(jnp.int32)
    col_pick = (col_ids[:, None] == every[None, :]).astype(jnp.int32)
    natural_rows = jnp.sum(row_pick * grid_order[None, :], axis=1)
    natural_cols = jnp.sum(col_pick * grid_order[None, :], axis=1)
    row_select = (natural_rows[:, None] == every[None, :]).astype(jnp.int32)
    listed = jnp.sum(row_select[:, :, None] * pattern[None, :, :], axis=1)
    hits = jnp.any(listed[:, :, None] == natural_cols[None, None, :], axis=1)
    return hits.astype(jnp.float32)


def fold_product(left, panel):
    return jnp.dot(
        lax.all_gather(left, "row", axis=1, tiled=True),
        panel,
        precision=lax.Precision.HIGHEST,
        preferred_element_type=jnp.float32,
    )


def panels(block, density, pattern, grid_order):
    row_count, col_count = density.shape
    row_blocks = row_count // block
    col_blocks = col_count // block
    first_row = lax.axis_index(("col", "rep")) * row_blocks
    first_col = lax.axis_index("row") * col_blocks
    hits = block_mask(pattern, grid_order, first_row, first_col, row_blocks, col_blocks)
    mask = jnp.broadcast_to(hits[:, None, :, None], (row_blocks, block, col_blocks, block)).reshape(
        row_count, col_count
    )
    current = density
    for repeat in range(STEPS):
        panel = lax.all_gather(current, ("col", "rep"), axis=0, tiled=True)
        square = fold_product(current, panel)
        cube = fold_product(square, panel)
        current = mask * (3.0 * square - 2.0 * cube)
    return current


def split(value):
    high = value.astype(jnp.bfloat16)
    low = (value - high.astype(jnp.float32)).astype(jnp.bfloat16)
    return high, low


def product(ah, al, bh, bl):
    dot = functools.partial(jnp.dot, preferred_element_type=jnp.float32)
    return dot(ah, bh) + (dot(ah, bl) + dot(al, bh))


def iotas(side):
    return (
        lax.broadcasted_iota(jnp.int32, (side, side), 0),
        lax.broadcasted_iota(jnp.int32, (side, side), 1),
    )


def pack_kernel(place_ref, x_ref, out_ref):
    side = x_ref.shape[0]
    big_row, core, big_col = place_ref[0], place_ref[1], place_ref[2]

    @pl.when(big_row != big_col)
    def _():
        pick = jnp.where(big_row < big_col, core, 1 - core)
        out_ref[:side, :] = x_ref[:, pl.ds(pl.multiple_of(pick * side, side), side)]
        out_ref[side:, :] = jnp.zeros((EXTRA, side), jnp.float32)

    @pl.when(big_row == big_col)
    def _():
        i, j = iotas(side)
        own = x_ref[:, pl.ds(pl.multiple_of(core * side, side), side)]
        other = x_ref[:, pl.ds(pl.multiple_of((1 - core) * side, side), side)]
        out_ref[:side, :] = jnp.where(i >= j, own, other)
        diagonal = jnp.sum(jnp.where(i == j, other, 0.0), axis=0, keepdims=True)
        out_ref[side:, :] = jnp.broadcast_to(diagonal, (EXTRA, side))


def work_kernel(sizes, place_ref, pattern_ref, order_ref, chunk_ref, out_ref, hits, xh, xl, zh, zl, ch, cl):
    rows_n, ranks = sizes
    side = chunk_ref.shape[-1]
    wide = 2 * side
    total = xh.shape[0]
    bigs = total // wide
    blocks = order_ref.shape[0]
    block = total // blocks
    big_row, core, big_col = place_ref[0], place_ref[1], place_ref[2]
    me = big_col * ranks + big_row * 2 + core

    lane_block = lax.broadcasted_iota(jnp.int32, (blocks, total), 1) // block
    row_block = lax.broadcasted_iota(jnp.int32, (blocks, total), 0)
    natural_col = jnp.zeros((blocks, total), jnp.int32)
    natural_row = jnp.zeros((blocks, total), jnp.int32)
    for b in range(blocks):
        natural_col = jnp.where(lane_block == b, order_ref[b], natural_col)
        natural_row = jnp.where(row_block == b, order_ref[b], natural_row)
    offset = natural_col - natural_row
    offset = jnp.where(offset < 0, offset + blocks, offset)
    hit = jnp.zeros((blocks, total), jnp.bool_)
    for k in range(pattern_ref.shape[1]):
        hit = hit | (offset == pattern_ref[0, k])
    hits[...] = hit.astype(jnp.float32)

    def position(device):
        away = me ^ device
        links = (ranks // 2).bit_length() - 1
        swapped = away & 1
        order = core ^ swapped
        spot = away // ranks
        for step in range(links):
            bit = jnp.where(order == 0, (away >> (1 + step)) & 1, (away >> (links - step)) & 1)
            spot = spot + bit * (rows_n << step)
        return spot + swapped * (rows_n << links)

    def put(h, l, value, r, c):
        high, low = split(value)
        h[r, c] = high
        l[r, c] = low

    def span(index, width):
        return slice(index * width, (index + 1) * width)

    for a in range(bigs):
        for b in range(bigs):
            if a == b:
                continue
            for j in range(2):
                k = j if a < b else 1 - j
                value = chunk_ref[position(b * ranks + a * 2 + j), :side, :]
                r, c = span(2 * a + j, side), span(2 * b + k, side)
                put(xh, xl, value, r, c)
                put(xh, xl, value.T, c, r)
    i, j = iotas(side)
    for a in range(bigs):
        p0 = position(a * ranks + a * 2)
        p1 = position(a * ranks + a * 2 + 1)
        m0 = chunk_ref[p0, :side, :]
        m1 = chunk_ref[p1, :side, :]
        diagonal = chunk_ref[p0, side : side + 1, :]
        t0, t1 = m0.T, m1.T
        r0, r1 = span(2 * a, side), span(2 * a + 1, side)
        put(xh, xl, jnp.where(i >= j, m0, t0), r0, r0)
        put(xh, xl, jnp.where(i >= j, m1, t1), r1, r1)
        put(xh, xl, jnp.where(i < j, m0, jnp.where(i > j, t1, diagonal)), r0, r1)
        put(xh, xl, jnp.where(i < j, m1, jnp.where(i > j, t0, diagonal)), r1, r0)

    def masked(value, first_block, cols):
        parts = []
        for b in range(value.shape[0] // block):
            parts.append(value[span(b, block)] * hits[pl.ds(first_block + b, 1), cols])
        return jnp.concatenate(parts, axis=0)

    for b in range(bigs):
        r, c = slice(0, (b + 1) * wide), span(b, wide)
        square = product(xh[r, :], xl[r, :], xh[:, c], xl[:, c])
        value = 3.0 * (xh[r, c].astype(jnp.float32) + xl[r, c].astype(jnp.float32)) - 2.0 * square
        put(zh, zl, value, r, c)
        if b:
            up = slice(0, b * wide)
            put(zh, zl, value[up].T, c, up)
    for b in range(bigs):
        r, c = slice(0, (b + 1) * wide), span(b, wide)
        value = masked(product(xh[r, :], xl[r, :], zh[:, c], zl[:, c]), 0, c)
        put(ch, cl, value, r, c)
        if b:
            up = slice(0, b * wide)
            put(ch, cl, value[up].T, c, up)

    cols = pl.ds(pl.multiple_of(big_col * wide, wide), wide)
    rows = pl.ds(pl.multiple_of((big_row * 2 + core) * side, side), side)
    wh, wl = ch[:, cols], cl[:, cols]
    square = product(ch[...], cl[...], wh, wl)
    value = 3.0 * (wh.astype(jnp.float32) + wl.astype(jnp.float32)) - 2.0 * square
    vh, vl = split(value)
    result = product(ch[rows, :], cl[rows, :], vh, vl)
    out_ref[...] = masked(result, (big_row * 2 + core) * (side // block), cols)


def whole(shape, density, pattern, grid_order):
    rows_n, cols_n, reps_n = (shape[name] for name in AXES)
    ranks = cols_n * reps_n
    side, wide = density.shape
    total = side * ranks

    def swap(value, partner):
        pairs = []
        for z in range(rows_n):
            for rank in range(ranks):
                z2, rank2 = partner(z, rank)
                pairs.append((z * ranks + rank, z2 * ranks + rank2))
        return lax.ppermute(value, AXES, pairs)

    rank = lax.axis_index(("col", "rep")).astype(jnp.int32)
    place = jnp.stack([rank // 2, rank % 2, lax.axis_index("row").astype(jnp.int32)])
    smem = pl.BlockSpec(memory_space=pltpu.SMEM)
    vmem = pl.BlockSpec(memory_space=pltpu.VMEM)
    mine = pl.pallas_call(
        pack_kernel,
        out_shape=jax.ShapeDtypeStruct((side + EXTRA, side), jnp.float32),
        in_specs=[smem, vmem],
        out_specs=vmem,
        name="pack",
    )(place, density)
    parts = [mine[None]]
    for away in range(1, rows_n):
        parts.append(swap(mine, lambda z, r, away=away: (z ^ away, r))[None])
    held = jnp.concatenate(parts, axis=0)
    links = (ranks // 2).bit_length() - 1
    for step in range(links):
        bits = (2 << step, 1 << (links - step))
        held = jnp.concatenate([held, swap(held, lambda z, r: (z, r ^ bits[r % 2]))], axis=0)
    held = jnp.concatenate([held, swap(held, lambda z, r: (z, r ^ 1))], axis=0)

    blocks = grid_order.shape[0]
    bf16 = pltpu.VMEM((total, total), jnp.bfloat16)
    return pl.pallas_call(
        functools.partial(work_kernel, (rows_n, ranks)),
        out_shape=jax.ShapeDtypeStruct((side, wide), jnp.float32),
        in_specs=[smem, smem, smem, vmem],
        out_specs=vmem,
        scratch_shapes=[pltpu.VMEM((blocks, total), jnp.float32)] + [bf16] * 6,
        compiler_params=pltpu.CompilerParams(vmem_limit_bytes=VMEM_BYTES),
        name="purify",
    )(place, pattern, grid_order, held)


def fits(shape, side, wide, total):
    sizes = [shape[name] for name in AXES]
    powers = all(size & (size - 1) == 0 for size in sizes)
    ranks = sizes[1] * sizes[2]
    squares = wide == 2 * side and side % 128 == 0 and sizes[0] * 2 == ranks
    return powers and squares and total * total * 24 <= VMEM_BYTES // 2 + 2**20


def solution(mesh):
    in_specs = (P(("col", "rep"), "row"), P(), P())
    out_specs = P(("col", "rep"), "row")
    shape = dict(mesh.shape)

    def local(density, pattern, grid_order):
        side, wide = density.shape
        total = side * shape["col"] * shape["rep"]
        if fits(shape, side, wide, total):
            return whole(shape, density, pattern, grid_order)
        return panels(total // grid_order.shape[0], density, pattern, grid_order)

    return jax.shard_map(local, mesh=mesh, in_specs=in_specs, out_specs=out_specs, check_vma=False)
```

```python
import functools

import jax
import jax.numpy as jnp
from jax import lax
from jax.experimental import pallas as pl
from jax.experimental.pallas import tpu as pltpu
from jax.sharding import PartitionSpec as P

STEPS = 2
AXES = ("row", "col", "rep")
PACK_BYTES = 2 * 2**20
WORK_BYTES = 28 * 2**20
EXTRA = 8


def block_mask(pattern, grid_order, first_row, first_col, row_blocks, col_blocks):
    total = grid_order.shape[0]
    every = jnp.arange(total, dtype=jnp.int32)
    row_ids = first_row + jnp.arange(row_blocks, dtype=jnp.int32)
    col_ids = first_col + jnp.arange(col_blocks, dtype=jnp.int32)
    row_pick = (row_ids[:, None] == every[None, :]).astype(jnp.int32)
    col_pick = (col_ids[:, None] == every[None, :]).astype(jnp.int32)
    natural_rows = jnp.sum(row_pick * grid_order[None, :], axis=1)
    natural_cols = jnp.sum(col_pick * grid_order[None, :], axis=1)
    row_select = (natural_rows[:, None] == every[None, :]).astype(jnp.int32)
    listed = jnp.sum(row_select[:, :, None] * pattern[None, :, :], axis=1)
    hits = jnp.any(listed[:, :, None] == natural_cols[None, None, :], axis=1)
    return hits.astype(jnp.float32)


def fold_product(left, panel):
    return jnp.dot(
        lax.all_gather(left, "row", axis=1, tiled=True),
        panel,
        precision=lax.Precision.HIGHEST,
        preferred_element_type=jnp.float32,
    )


def panels(block, density, pattern, grid_order):
    row_count, col_count = density.shape
    row_blocks = row_count // block
    col_blocks = col_count // block
    first_row = lax.axis_index(("col", "rep")) * row_blocks
    first_col = lax.axis_index("row") * col_blocks
    hits = block_mask(pattern, grid_order, first_row, first_col, row_blocks, col_blocks)
    mask = jnp.broadcast_to(hits[:, None, :, None], (row_blocks, block, col_blocks, block)).reshape(
        row_count, col_count
    )
    current = density
    for repeat in range(STEPS):
        panel = lax.all_gather(current, ("col", "rep"), axis=0, tiled=True)
        square = fold_product(current, panel)
        cube = fold_product(square, panel)
        current = mask * (3.0 * square - 2.0 * cube)
    return current


def split(value):
    high = value.astype(jnp.bfloat16)
    low = (value - high.astype(jnp.float32)).astype(jnp.bfloat16)
    return high, low


def product(ah, al, bh, bl):
    dot = functools.partial(jnp.dot, preferred_element_type=jnp.float32)
    return dot(ah, bh) + (dot(ah, bl) + dot(al, bh))


def iotas(side):
    return (
        lax.broadcasted_iota(jnp.int32, (side, side), 0),
        lax.broadcasted_iota(jnp.int32, (side, side), 1),
    )


def place(reps_n):
    rank = lax.axis_index("col") * reps_n + lax.axis_index("rep")
    return rank // 2, rank & 1, lax.axis_index("row")


def pack_kernel(reps_n, x_ref, out_ref):
    side = x_ref.shape[0]
    big_row, core, big_col = place(reps_n)

    @pl.when(big_row != big_col)
    def _():
        pick = jnp.where(big_row < big_col, core, 1 - core)
        out_ref[:side, :] = x_ref[:, pl.ds(pl.multiple_of(pick * side, side), side)]
        out_ref[side:, :] = jnp.zeros((EXTRA, side), jnp.float32)

    @pl.when(big_row == big_col)
    def _():
        i, j = iotas(side)
        own = x_ref[:, pl.ds(pl.multiple_of(core * side, side), side)]
        other = x_ref[:, pl.ds(pl.multiple_of((1 - core) * side, side), side)]
        out_ref[:side, :] = jnp.where(i >= j, own, other)
        diagonal = jnp.sum(jnp.where(i == j, other, 0.0), axis=0, keepdims=True)
        out_ref[side:, :] = jnp.broadcast_to(diagonal, (EXTRA, side))


def work_kernel(sizes, pattern_ref, order_ref, near_ref, far_ref, out_ref, hits, xh, xl, zh, zl, ch, cl):
    rows_n, ranks, reps_n = sizes
    side = near_ref.shape[-1]
    wide = 2 * side
    total = xh.shape[0]
    bigs = total // wide
    blocks = order_ref.shape[0]
    block = total // blocks
    big_row, core, big_col = place(reps_n)
    me = big_col * ranks + big_row * 2 + core

    lane_block = lax.broadcasted_iota(jnp.int32, (blocks, total), 1) // block
    row_block = lax.broadcasted_iota(jnp.int32, (blocks, total), 0)
    natural_col = jnp.zeros((blocks, total), jnp.int32)
    natural_row = jnp.zeros((blocks, total), jnp.int32)
    for b in range(blocks):
        natural_col = jnp.where(lane_block == b, order_ref[b], natural_col)
        natural_row = jnp.where(row_block == b, order_ref[b], natural_row)
    offset = natural_col - natural_row
    offset = jnp.where(offset < 0, offset + blocks, offset)
    hit = jnp.zeros((blocks, total), jnp.bool_)
    for k in range(pattern_ref.shape[1]):
        hit = hit | (offset == pattern_ref[0, k])
    hits[...] = hit.astype(jnp.float32)

    def position(device):
        away = me ^ device
        half_n = rows_n // 2
        links = (ranks // 2).bit_length() - 1
        swapped = away & 1
        order = core ^ swapped
        spot = (away // ranks) % half_n
        for step in range(links):
            bit = jnp.where(order == 0, (away >> (1 + step)) & 1, (away >> (links - step)) & 1)
            spot = spot + bit * (half_n << step)
        return away // ranks >= half_n, spot + swapped * (half_n << links)

    def chunk(device, rows):
        far, spot = position(device)
        return jnp.where(far, far_ref[spot, rows, :], near_ref[spot, rows, :])

    def put(h, l, value, r, c):
        high, low = split(value)
        h[r, c] = high
        l[r, c] = low

    def span(index, width):
        return slice(index * width, (index + 1) * width)

    for a in range(bigs):
        for b in range(bigs):
            if a == b:
                continue
            for j in range(2):
                k = j if a < b else 1 - j
                value = chunk(b * ranks + a * 2 + j, slice(0, side))
                r, c = span(2 * a + j, side), span(2 * b + k, side)
                put(xh, xl, value, r, c)
                put(xh, xl, value.T, c, r)
    i, j = iotas(side)
    for a in range(bigs):
        first = a * ranks + a * 2
        m0 = chunk(first, slice(0, side))
        m1 = chunk(first + 1, slice(0, side))
        diagonal = chunk(first, slice(side, side + 1))
        t0, t1 = m0.T, m1.T
        r0, r1 = span(2 * a, side), span(2 * a + 1, side)
        put(xh, xl, jnp.where(i >= j, m0, t0), r0, r0)
        put(xh, xl, jnp.where(i >= j, m1, t1), r1, r1)
        put(xh, xl, jnp.where(i < j, m0, jnp.where(i > j, t1, diagonal)), r0, r1)
        put(xh, xl, jnp.where(i < j, m1, jnp.where(i > j, t0, diagonal)), r1, r0)

    def masked(value, first_block, cols):
        parts = []
        for b in range(value.shape[0] // block):
            parts.append(value[span(b, block)] * hits[pl.ds(first_block + b, 1), cols])
        return jnp.concatenate(parts, axis=0)

    for b in reversed(range(bigs)):
        r, c = slice(0, (b + 1) * wide), span(b, wide)
        square = product(xh[r, :], xl[r, :], xh[:, c], xl[:, c])
        value = 3.0 * (xh[r, c].astype(jnp.float32) + xl[r, c].astype(jnp.float32)) - 2.0 * square
        put(zh, zl, value, r, c)
        if b:
            up = slice(0, b * wide)
            put(zh, zl, value[up].T, c, up)
    cols = pl.ds(pl.multiple_of(big_col * wide, wide), wide)
    rank = big_row * 2 + core
    rows = pl.ds(pl.multiple_of(rank * side, side), side)
    late = slice(wide, total)
    for b in reversed(range(bigs)):
        if b == 0:
            partial = product(ch[:, late], cl[:, late], ch[late, cols], cl[late, cols])
        r, c = slice(0, (b + 1) * wide), span(b, wide)
        value = masked(product(xh[r, :], xl[r, :], zh[:, c], zl[:, c]), 0, c)
        put(ch, cl, value, r, c)
        if b:
            up = slice(0, b * wide)
            put(ch, cl, value[up].T, c, up)

    first = slice(0, wide)
    result = jnp.zeros((side, wide), jnp.float32)
    for b in range(bigs):
        r = span(b, wide)
        square = partial[r] + product(ch[r, first], cl[r, first], ch[first, cols], cl[first, cols])
        value = 3.0 * (ch[r, cols].astype(jnp.float32) + cl[r, cols].astype(jnp.float32)) - 2.0 * square
        vh, vl = split(value)
        result = result + product(ch[rows, r], cl[rows, r], vh, vl)
    out_ref[...] = masked(result, rank * (side // block), cols)


def whole(shape, density, pattern, grid_order):
    rows_n, cols_n, reps_n = (shape[name] for name in AXES)
    ranks = cols_n * reps_n
    side, wide = density.shape
    total = side * ranks

    def swap(value, partner):
        pairs = []
        for z in range(rows_n):
            for rank in range(ranks):
                z2, rank2 = partner(z, rank)
                pairs.append((z * ranks + rank, z2 * ranks + rank2))
        return lax.ppermute(value, AXES, pairs)

    smem = pl.BlockSpec(memory_space=pltpu.SMEM)
    vmem = pl.BlockSpec(memory_space=pltpu.VMEM)
    mine = pl.pallas_call(
        functools.partial(pack_kernel, reps_n),
        out_shape=jax.ShapeDtypeStruct((side + EXTRA, side), jnp.float32),
        in_specs=[vmem],
        out_specs=vmem,
        compiler_params=pltpu.CompilerParams(vmem_limit_bytes=PACK_BYTES),
        name="pack",
    )(density)
    parts = [mine[None]]
    for away in range(1, rows_n):
        parts.append(swap(mine, lambda z, r, away=away: (z ^ away, r))[None])
    links = (ranks // 2).bit_length() - 1
    held = []
    for half in (parts[: rows_n // 2], parts[rows_n // 2 :]):
        value = jnp.concatenate(half, axis=0)
        for step in range(links):
            bits = (2 << step, 1 << (links - step))
            value = jnp.concatenate([value, swap(value, lambda z, r: (z, r ^ bits[r % 2]))], axis=0)
        held.append(jnp.concatenate([value, swap(value, lambda z, r: (z, r ^ 1))], axis=0))

    blocks = grid_order.shape[0]
    bf16 = pltpu.VMEM((total, total), jnp.bfloat16)
    return pl.pallas_call(
        functools.partial(work_kernel, (rows_n, ranks, reps_n)),
        out_shape=jax.ShapeDtypeStruct((side, wide), jnp.float32),
        in_specs=[smem, smem, vmem, vmem],
        out_specs=vmem,
        scratch_shapes=[pltpu.VMEM((blocks, total), jnp.float32)] + [bf16] * 6,
        compiler_params=pltpu.CompilerParams(vmem_limit_bytes=WORK_BYTES),
        name="purify",
    )(pattern, grid_order, *held)


def fits(shape, side, wide, total):
    sizes = [shape[name] for name in AXES]
    powers = all(size & (size - 1) == 0 for size in sizes)
    ranks = sizes[1] * sizes[2]
    squares = wide == 2 * side and side % 128 == 0 and sizes[0] * 2 == ranks
    return powers and squares and total * total * 24 <= WORK_BYTES


def solution(mesh):
    in_specs = (P(("col", "rep"), "row"), P(), P())
    out_specs = P(("col", "rep"), "row")
    shape = dict(mesh.shape)

    def local(density, pattern, grid_order):
        side, wide = density.shape
        total = side * shape["col"] * shape["rep"]
        if fits(shape, side, wide, total):
            return whole(shape, density, pattern, grid_order)
        return panels(total // grid_order.shape[0], density, pattern, grid_order)

    return jax.shard_map(local, mesh=mesh, in_specs=in_specs, out_specs=out_specs, check_vma=False)
```

```python
import functools

import jax
import jax.numpy as jnp
from jax import lax
from jax.experimental import pallas as pl
from jax.experimental.pallas import tpu as pltpu
from jax.sharding import PartitionSpec as P

STEPS = 2
AXES = ("row", "col", "rep")
PACK_BYTES = 2 * 2**20
WORK_BYTES = 28 * 2**20
EXTRA = 8


def block_mask(pattern, grid_order, first_row, first_col, row_blocks, col_blocks):
    total = grid_order.shape[0]
    every = jnp.arange(total, dtype=jnp.int32)
    row_ids = first_row + jnp.arange(row_blocks, dtype=jnp.int32)
    col_ids = first_col + jnp.arange(col_blocks, dtype=jnp.int32)
    row_pick = (row_ids[:, None] == every[None, :]).astype(jnp.int32)
    col_pick = (col_ids[:, None] == every[None, :]).astype(jnp.int32)
    natural_rows = jnp.sum(row_pick * grid_order[None, :], axis=1)
    natural_cols = jnp.sum(col_pick * grid_order[None, :], axis=1)
    row_select = (natural_rows[:, None] == every[None, :]).astype(jnp.int32)
    listed = jnp.sum(row_select[:, :, None] * pattern[None, :, :], axis=1)
    hits = jnp.any(listed[:, :, None] == natural_cols[None, None, :], axis=1)
    return hits.astype(jnp.float32)


def fold_product(left, panel):
    return jnp.dot(
        lax.all_gather(left, "row", axis=1, tiled=True),
        panel,
        precision=lax.Precision.HIGHEST,
        preferred_element_type=jnp.float32,
    )


def panels(block, density, pattern, grid_order):
    row_count, col_count = density.shape
    row_blocks = row_count // block
    col_blocks = col_count // block
    first_row = lax.axis_index(("col", "rep")) * row_blocks
    first_col = lax.axis_index("row") * col_blocks
    hits = block_mask(pattern, grid_order, first_row, first_col, row_blocks, col_blocks)
    mask = jnp.broadcast_to(hits[:, None, :, None], (row_blocks, block, col_blocks, block)).reshape(
        row_count, col_count
    )
    current = density
    for repeat in range(STEPS):
        panel = lax.all_gather(current, ("col", "rep"), axis=0, tiled=True)
        square = fold_product(current, panel)
        cube = fold_product(square, panel)
        current = mask * (3.0 * square - 2.0 * cube)
    return current


def split(value):
    high = value.astype(jnp.bfloat16)
    low = (value - high.astype(jnp.float32)).astype(jnp.bfloat16)
    return high, low


def product(ah, al, bh, bl):
    left = jnp.concatenate([ah, ah, al], axis=1)
    right = jnp.concatenate([bh, bl, bh], axis=0)
    return jnp.dot(left, right, preferred_element_type=jnp.float32)


def iotas(side):
    return (
        lax.broadcasted_iota(jnp.int32, (side, side), 0),
        lax.broadcasted_iota(jnp.int32, (side, side), 1),
    )


def place(reps_n):
    rank = lax.axis_index("col") * reps_n + lax.axis_index("rep")
    return rank // 2, rank & 1, lax.axis_index("row")


def pack_kernel(reps_n, x_ref, out_ref):
    side = x_ref.shape[0]
    big_row, core, big_col = place(reps_n)

    @pl.when(big_row != big_col)
    def _():
        pick = jnp.where(big_row < big_col, core, 1 - core)
        out_ref[:side, :] = x_ref[:, pl.ds(pl.multiple_of(pick * side, side), side)]
        out_ref[side:, :] = jnp.zeros((EXTRA, side), jnp.float32)

    @pl.when(big_row == big_col)
    def _():
        i, j = iotas(side)
        own = x_ref[:, pl.ds(pl.multiple_of(core * side, side), side)]
        other = x_ref[:, pl.ds(pl.multiple_of((1 - core) * side, side), side)]
        out_ref[:side, :] = jnp.where(i >= j, own, other)
        diagonal = jnp.sum(jnp.where(i == j, other, 0.0), axis=0, keepdims=True)
        out_ref[side:, :] = jnp.broadcast_to(diagonal, (EXTRA, side))


def write_mask(pattern_ref, order_ref, hits):
    blocks, total = hits.shape
    lane_block = lax.broadcasted_iota(jnp.int32, (1, total), 1) // (total // blocks)
    row_block = lax.broadcasted_iota(jnp.int32, (blocks, 1), 0)
    natural_col = jnp.zeros((1, total), jnp.int32)
    natural_row = jnp.zeros((blocks, 1), jnp.int32)
    for b in range(blocks):
        natural = order_ref[:, b : b + 1]
        natural_col = jnp.where(lane_block == b, natural, natural_col)
        natural_row = jnp.where(row_block == b, natural, natural_row)
    offset = natural_col - natural_row
    offset = jnp.where(offset < 0, offset + blocks, offset)
    hit = jnp.zeros((blocks, total), jnp.bool_)
    for k in range(pattern_ref.shape[1]):
        hit = hit | (offset == pattern_ref[0:1, k : k + 1])
    hits[...] = hit.astype(jnp.float32)


def work_kernel(sizes, held, pattern_ref, order_ref, out_ref, hits, xh, xl, zh, zl, ch, cl):
    rows_n, ranks, reps_n = sizes
    side = held.shape[-1]
    wide = 2 * side
    total = xh.shape[0]
    bigs = total // wide
    blocks = hits.shape[0]
    block = total // blocks
    big_row, core, big_col = place(reps_n)
    links = (ranks // 2).bit_length() - 1

    rank = big_row * 2 + core

    def chunk(a, core_of, b, rows):
        away = rank ^ (a * 2 + core_of)
        swapped = away & 1
        order = core ^ swapped
        spot = (big_col ^ b) * ranks + (swapped << links)
        for step in range(links):
            bit = jnp.where(order == 0, (away >> (1 + step)) & 1, (away >> (links - step)) & 1)
            spot = spot + (bit << step)
        return held[spot, rows, :]

    def put(h, l, value, r, c):
        high, low = split(value)
        h[r, c] = high
        l[r, c] = low

    def span(index, width):
        return slice(index * width, (index + 1) * width)

    def at(index, width):
        return pl.ds(pl.multiple_of(index * width, width), width)

    def unpack(a, b):
        if a != b:
            for j in range(2):
                k = j if a < b else 1 - j
                value = chunk(a, j, b, slice(0, side))
                r, c = span(2 * a + j, side), span(2 * b + k, side)
                put(xh, xl, value, r, c)
                put(xh, xl, value.T, c, r)
            return
        i, j = iotas(side)
        m0 = chunk(a, 0, a, slice(0, side))
        m1 = chunk(a, 1, a, slice(0, side))
        diagonal = chunk(a, 0, a, slice(side, side + 1))
        t0, t1 = m0.T, m1.T
        r0, r1 = span(2 * a, side), span(2 * a + 1, side)
        put(xh, xl, jnp.where(i >= j, m0, t0), r0, r0)
        put(xh, xl, jnp.where(i >= j, m1, t1), r1, r1)
        put(xh, xl, jnp.where(i < j, m0, jnp.where(i > j, t1, diagonal)), r0, r1)
        put(xh, xl, jnp.where(i < j, m1, jnp.where(i > j, t0, diagonal)), r1, r0)

    def masked(value, first_block, cols):
        parts = []
        for b in range(value.shape[0] // block):
            parts.append(value[span(b, block)] * hits[pl.ds(first_block + b, 1), cols])
        return jnp.concatenate(parts, axis=0)

    def mirrored(h, l, value, a, b):
        put(h, l, value, span(a, wide), span(b, wide))
        if a != b:
            put(h, l, value.T, span(b, wide), span(a, wide))

    write_mask(pattern_ref, order_ref, hits)

    for b in reversed(range(bigs)):
        for a in reversed(range(b + 1)):
            r, c = span(a, wide), span(b, wide)
            if b == bigs - 1:
                for k in range(a, -1, -1):
                    unpack(a, k)
                    if a != k:
                        unpack(k, a)
            square = product(xh[r, :], xl[r, :], xh[:, c], xl[:, c])
            value = 3.0 * (xh[r, c].astype(jnp.float32) + xl[r, c].astype(jnp.float32)) - 2.0 * square
            mirrored(zh, zl, value, a, b)

    cols = at(big_col, wide)
    rows = at(rank, side)

    def term(k):
        r = span(k, wide)
        return product(ch[rows, r], cl[rows, r], ch[r, :], cl[r, :])

    square = None
    for b in reversed(range(bigs)):
        for a in reversed(range(b + 1)):
            r, c = span(a, wide), span(b, wide)
            value = product(xh[r, :], xl[r, :], zh[:, c], zl[:, c])
            if a == 0 and b + 1 < bigs:
                square = term(b + 1) if square is None else square + term(b + 1)
            mirrored(ch, cl, masked(value, a * (wide // block), c), a, b)
    square = square + term(0)
    value = 3.0 * (ch[rows, :].astype(jnp.float32) + cl[rows, :].astype(jnp.float32)) - 2.0 * square
    vh, vl = split(value)
    result = product(vh, vl, ch[:, cols], cl[:, cols])
    out_ref[...] = masked(result, rank * (side // block), cols)


def whole(shape, density, pattern, grid_order):
    rows_n, cols_n, reps_n = (shape[name] for name in AXES)
    ranks = cols_n * reps_n
    side, wide = density.shape
    total = side * ranks

    def swap(value, partner):
        pairs = []
        for z in range(rows_n):
            for rank in range(ranks):
                z2, rank2 = partner(z, rank)
                pairs.append((z * ranks + rank, z2 * ranks + rank2))
        return lax.ppermute(value, AXES, pairs)

    vmem = pl.BlockSpec(memory_space=pltpu.VMEM)
    mine = pl.pallas_call(
        functools.partial(pack_kernel, reps_n),
        out_shape=jax.ShapeDtypeStruct((side + EXTRA, side), jnp.float32),
        in_specs=[vmem],
        out_specs=vmem,
        compiler_params=pltpu.CompilerParams(vmem_limit_bytes=PACK_BYTES),
        name="pack",
    )(density)
    links = (ranks // 2).bit_length() - 1
    held = []
    for away in range(rows_n):
        value = (swap(mine, lambda z, r: (z ^ away, r)) if away else mine)[None]
        for step in range(links):
            bits = (2 << step, 1 << (links - step))
            value = jnp.concatenate([value, swap(value, lambda z, r: (z, r ^ bits[r % 2]))], axis=0)
        held += [value, swap(value, lambda z, r: (z, r ^ 1))]

    return pl.pallas_call(
        functools.partial(work_kernel, (rows_n, ranks, reps_n)),
        out_shape=jax.ShapeDtypeStruct((side, wide), jnp.float32),
        in_specs=[vmem] * 3,
        out_specs=vmem,
        scratch_shapes=[pltpu.VMEM((grid_order.shape[0], total), jnp.float32)]
        + [pltpu.VMEM((total, total), jnp.bfloat16)] * 6,
        compiler_params=pltpu.CompilerParams(vmem_limit_bytes=WORK_BYTES),
        name="purify",
    )(jnp.concatenate(held, axis=0), pattern, grid_order[None])


def fits(shape, side, wide, total):
    sizes = [shape[name] for name in AXES]
    powers = all(size & (size - 1) == 0 for size in sizes)
    ranks = sizes[1] * sizes[2]
    squares = wide == 2 * side and side % 128 == 0 and sizes[0] * 2 == ranks
    return powers and squares and total * total * 24 <= WORK_BYTES


def solution(mesh):
    in_specs = (P(("col", "rep"), "row"), P(), P())
    out_specs = P(("col", "rep"), "row")
    shape = dict(mesh.shape)

    def local(density, pattern, grid_order):
        side, wide = density.shape
        total = side * shape["col"] * shape["rep"]
        if fits(shape, side, wide, total):
            return whole(shape, density, pattern, grid_order)
        return panels(total // grid_order.shape[0], density, pattern, grid_order)

    return jax.shard_map(local, mesh=mesh, in_specs=in_specs, out_specs=out_specs, check_vma=False)
```

```python
import functools

import jax
import jax.numpy as jnp
from jax import lax
from jax.experimental import pallas as pl
from jax.experimental.pallas import tpu as pltpu
from jax.sharding import PartitionSpec as P

STEPS = 2
AXES = ("row", "col", "rep")
PACK_BYTES = 2 * 2**20
WORK_BYTES = 28 * 2**20
FLIPPED = 0b0011
EXTRA = 8


def block_mask(pattern, grid_order, first_row, first_col, row_blocks, col_blocks):
    total = grid_order.shape[0]
    every = jnp.arange(total, dtype=jnp.int32)
    row_ids = first_row + jnp.arange(row_blocks, dtype=jnp.int32)
    col_ids = first_col + jnp.arange(col_blocks, dtype=jnp.int32)
    row_pick = (row_ids[:, None] == every[None, :]).astype(jnp.int32)
    col_pick = (col_ids[:, None] == every[None, :]).astype(jnp.int32)
    natural_rows = jnp.sum(row_pick * grid_order[None, :], axis=1)
    natural_cols = jnp.sum(col_pick * grid_order[None, :], axis=1)
    row_select = (natural_rows[:, None] == every[None, :]).astype(jnp.int32)
    listed = jnp.sum(row_select[:, :, None] * pattern[None, :, :], axis=1)
    hits = jnp.any(listed[:, :, None] == natural_cols[None, None, :], axis=1)
    return hits.astype(jnp.float32)


def fold_product(left, panel):
    return jnp.dot(
        lax.all_gather(left, "row", axis=1, tiled=True),
        panel,
        precision=lax.Precision.HIGHEST,
        preferred_element_type=jnp.float32,
    )


def panels(block, density, pattern, grid_order):
    row_count, col_count = density.shape
    row_blocks = row_count // block
    col_blocks = col_count // block
    first_row = lax.axis_index(("col", "rep")) * row_blocks
    first_col = lax.axis_index("row") * col_blocks
    hits = block_mask(pattern, grid_order, first_row, first_col, row_blocks, col_blocks)
    mask = jnp.broadcast_to(hits[:, None, :, None], (row_blocks, block, col_blocks, block)).reshape(
        row_count, col_count
    )
    current = density
    for repeat in range(STEPS):
        panel = lax.all_gather(current, ("col", "rep"), axis=0, tiled=True)
        square = fold_product(current, panel)
        cube = fold_product(square, panel)
        current = mask * (3.0 * square - 2.0 * cube)
    return current


def split(value):
    high = value.astype(jnp.bfloat16)
    low = (value - high.astype(jnp.float32)).astype(jnp.bfloat16)
    return high, low


def product(ah, al, bh, bl):
    left = jnp.concatenate([ah, ah, al], axis=1)
    right = jnp.concatenate([bh, bl, bh], axis=0)
    return jnp.dot(left, right, preferred_element_type=jnp.float32)


def iotas(side):
    return (
        lax.broadcasted_iota(jnp.int32, (side, side), 0),
        lax.broadcasted_iota(jnp.int32, (side, side), 1),
    )


def place(reps_n):
    rank = lax.axis_index("col") * reps_n + lax.axis_index("rep")
    return rank // 2, rank & 1, lax.axis_index("row")


def pack_kernel(reps_n, x_ref, out_ref):
    side = x_ref.shape[0]
    big_row, core, big_col = place(reps_n)

    @pl.when(big_row != big_col)
    def _():
        pick = jnp.where(big_row < big_col, core, 1 - core)
        out_ref[:side, :] = x_ref[:, pl.ds(pl.multiple_of(pick * side, side), side)]
        out_ref[side:, :] = jnp.zeros((EXTRA, side), jnp.float32)

    @pl.when(big_row == big_col)
    def _():
        i, j = iotas(side)
        own = x_ref[:, pl.ds(pl.multiple_of(core * side, side), side)]
        other = x_ref[:, pl.ds(pl.multiple_of((1 - core) * side, side), side)]
        out_ref[:side, :] = jnp.where(i >= j, own, other)
        diagonal = jnp.sum(jnp.where(i == j, other, 0.0), axis=0, keepdims=True)
        out_ref[side:, :] = jnp.broadcast_to(diagonal, (EXTRA, side))


def write_mask(pattern_ref, order_ref, hits):
    blocks, total = hits.shape
    lane_block = lax.broadcasted_iota(jnp.int32, (1, total), 1) // (total // blocks)
    row_block = lax.broadcasted_iota(jnp.int32, (blocks, 1), 0)
    natural_col = jnp.zeros((1, total), jnp.int32)
    natural_row = jnp.zeros((blocks, 1), jnp.int32)
    for b in range(blocks):
        natural = order_ref[:, b : b + 1]
        natural_col = jnp.where(lane_block == b, natural, natural_col)
        natural_row = jnp.where(row_block == b, natural, natural_row)
    offset = natural_col - natural_row
    offset = jnp.where(offset < 0, offset + blocks, offset)
    hit = jnp.zeros((blocks, total), jnp.bool_)
    for k in range(pattern_ref.shape[1]):
        hit = hit | (offset == pattern_ref[0:1, k : k + 1])
    hits[...] = hit.astype(jnp.float32)


def work_kernel(sizes, held, pattern_ref, order_ref, out_ref, hits, xh, xl, zh, zl, ch, cl):
    rows_n, ranks, reps_n = sizes
    side = held.shape[-1]
    wide = 2 * side
    total = xh.shape[0]
    bigs = total // wide
    blocks = hits.shape[0]
    block = total // blocks
    big_row, core, big_col = place(reps_n)
    links = (ranks // 2).bit_length() - 1

    rank = big_row * 2 + core

    def chunk(a, core_of, b, rows):
        away = rank ^ (a * 2 + core_of)
        swapped = away & 1
        chain = big_col ^ b
        order = core ^ swapped ^ ((FLIPPED >> chain) & 1)
        spot = chain * ranks + (swapped << links)
        for step in range(links):
            bit = jnp.where(order == 0, (away >> (1 + step)) & 1, (away >> (links - step)) & 1)
            spot = spot + (bit << step)
        return held[spot, rows, :]

    def put(h, l, value, r, c):
        high, low = split(value)
        h[r, c] = high
        l[r, c] = low

    def span(index, width):
        return slice(index * width, (index + 1) * width)

    def at(index, width):
        return pl.ds(pl.multiple_of(index * width, width), width)

    def unpack(a, b):
        if a != b:
            for j in range(2):
                k = j if a < b else 1 - j
                value = chunk(a, j, b, slice(0, side))
                r, c = span(2 * a + j, side), span(2 * b + k, side)
                put(xh, xl, value, r, c)
                put(xh, xl, value.T, c, r)
            return
        i, j = iotas(side)
        m0 = chunk(a, 0, a, slice(0, side))
        m1 = chunk(a, 1, a, slice(0, side))
        diagonal = chunk(a, 0, a, slice(side, side + 1))
        t0, t1 = m0.T, m1.T
        r0, r1 = span(2 * a, side), span(2 * a + 1, side)
        put(xh, xl, jnp.where(i >= j, m0, t0), r0, r0)
        put(xh, xl, jnp.where(i >= j, m1, t1), r1, r1)
        put(xh, xl, jnp.where(i < j, m0, jnp.where(i > j, t1, diagonal)), r0, r1)
        put(xh, xl, jnp.where(i < j, m1, jnp.where(i > j, t0, diagonal)), r1, r0)

    def masked(value, first_block, cols):
        parts = []
        for b in range(value.shape[0] // block):
            parts.append(value[span(b, block)] * hits[pl.ds(first_block + b, 1), cols])
        return jnp.concatenate(parts, axis=0)

    def mirrored(h, l, value, a, b):
        put(h, l, value, span(a, wide), span(b, wide))
        if a != b:
            put(h, l, value.T, span(b, wide), span(a, wide))

    write_mask(pattern_ref, order_ref, hits)

    for b in reversed(range(bigs)):
        for a in reversed(range(b + 1)):
            r, c = span(a, wide), span(b, wide)
            if b == bigs - 1:
                for k in range(a, -1, -1):
                    unpack(a, k)
                    if a != k:
                        unpack(k, a)
            if a == b:
                both = jnp.dot(
                    xh[r, :],
                    jnp.concatenate([xh[:, c], xl[:, c]], axis=1),
                    preferred_element_type=jnp.float32,
                )
                square = both[:, :wide] + (both[:, wide:] + both[:, wide:].T)
            else:
                square = product(xh[r, :], xl[r, :], xh[:, c], xl[:, c])
            value = 3.0 * (xh[r, c].astype(jnp.float32) + xl[r, c].astype(jnp.float32)) - 2.0 * square
            mirrored(zh, zl, value, a, b)

    cols = at(big_col, wide)
    rows = at(rank, side)

    def term(k):
        r = span(k, wide)
        return product(ch[rows, r], cl[rows, r], ch[r, :], cl[r, :])

    square = None
    for b in reversed(range(bigs)):
        for a in reversed(range(b + 1)):
            r, c = span(a, wide), span(b, wide)
            value = product(xh[r, :], xl[r, :], zh[:, c], zl[:, c])
            if a == 0 and b + 1 < bigs:
                square = term(b + 1) if square is None else square + term(b + 1)
            mirrored(ch, cl, masked(value, a * (wide // block), c), a, b)
    square = square + term(0)
    value = 3.0 * (ch[rows, :].astype(jnp.float32) + cl[rows, :].astype(jnp.float32)) - 2.0 * square
    vh, vl = split(value)
    result = product(vh, vl, ch[:, cols], cl[:, cols])
    out_ref[...] = masked(result, rank * (side // block), cols)


def whole(shape, density, pattern, grid_order):
    rows_n, cols_n, reps_n = (shape[name] for name in AXES)
    ranks = cols_n * reps_n
    side, wide = density.shape
    total = side * ranks

    def swap(value, partner):
        pairs = []
        for z in range(rows_n):
            for rank in range(ranks):
                z2, rank2 = partner(z, rank)
                pairs.append((z * ranks + rank, z2 * ranks + rank2))
        return lax.ppermute(value, AXES, pairs)

    vmem = pl.BlockSpec(memory_space=pltpu.VMEM)
    mine = pl.pallas_call(
        functools.partial(pack_kernel, reps_n),
        out_shape=jax.ShapeDtypeStruct((side + EXTRA, side), jnp.float32),
        in_specs=[vmem],
        out_specs=vmem,
        compiler_params=pltpu.CompilerParams(vmem_limit_bytes=PACK_BYTES),
        name="pack",
    )(density)
    links = (ranks // 2).bit_length() - 1
    chains = [*range(1, rows_n, 2), *range(rows_n - 2, 0, -2)]
    value, last = [mine[None]] * rows_n, None
    for z_away in chains:
        value[z_away] = swap(mine, lambda z, r: (z ^ z_away, r))[None]
    for step in range(links):
        for chain in [*chains, 0]:
            if step and not chain:
                value[0], last = lax.optimization_barrier((value[0], last))
            bits = (2 << step, 1 << (links - step))
            flip = FLIPPED >> chain & 1
            came = swap(value[chain], lambda z, r: (z, r ^ bits[r % 2 ^ flip]))
            value[chain] = jnp.concatenate([value[chain], came], axis=0)
            last = came if not step and chain == rows_n - 1 else last
    held = []
    for chain in range(rows_n):
        held += [value[chain], swap(value[chain], lambda z, r: (z, r ^ 1))]

    return pl.pallas_call(
        functools.partial(work_kernel, (rows_n, ranks, reps_n)),
        out_shape=jax.ShapeDtypeStruct((side, wide), jnp.float32),
        in_specs=[vmem] * 3,
        out_specs=vmem,
        scratch_shapes=[pltpu.VMEM((grid_order.shape[0], total), jnp.float32)]
        + [pltpu.VMEM((total, total), jnp.bfloat16)] * 6,
        compiler_params=pltpu.CompilerParams(vmem_limit_bytes=WORK_BYTES),
        name="purify",
    )(jnp.concatenate(held, axis=0), pattern, grid_order[None])


def fits(shape, side, wide, total):
    sizes = [shape[name] for name in AXES]
    powers = all(size & (size - 1) == 0 for size in sizes)
    ranks = sizes[1] * sizes[2]
    squares = wide == 2 * side and side % 128 == 0 and sizes[0] * 2 == ranks
    return powers and squares and total * total * 24 <= WORK_BYTES


def solution(mesh):
    in_specs = (P(("col", "rep"), "row"), P(), P())
    out_specs = P(("col", "rep"), "row")
    shape = dict(mesh.shape)

    def local(density, pattern, grid_order):
        side, wide = density.shape
        total = side * shape["col"] * shape["rep"]
        if fits(shape, side, wide, total):
            return whole(shape, density, pattern, grid_order)
        return panels(total // grid_order.shape[0], density, pattern, grid_order)

    return jax.shard_map(local, mesh=mesh, in_specs=in_specs, out_specs=out_specs, check_vma=False)
```

```python
import functools

import jax
import jax.numpy as jnp
from jax import lax
from jax.experimental import pallas as pl
from jax.experimental.pallas import tpu as pltpu
from jax.sharding import PartitionSpec as P

STEPS = 2
AXES = ("row", "col", "rep")
PACK_BYTES = 2 * 2**20
WORK_BYTES = 28 * 2**20
EXTRA = 8


def block_mask(pattern, grid_order, first_row, first_col, row_blocks, col_blocks):
    total = grid_order.shape[0]
    every = jnp.arange(total, dtype=jnp.int32)
    row_ids = first_row + jnp.arange(row_blocks, dtype=jnp.int32)
    col_ids = first_col + jnp.arange(col_blocks, dtype=jnp.int32)
    row_pick = (row_ids[:, None] == every[None, :]).astype(jnp.int32)
    col_pick = (col_ids[:, None] == every[None, :]).astype(jnp.int32)
    natural_rows = jnp.sum(row_pick * grid_order[None, :], axis=1)
    natural_cols = jnp.sum(col_pick * grid_order[None, :], axis=1)
    row_select = (natural_rows[:, None] == every[None, :]).astype(jnp.int32)
    listed = jnp.sum(row_select[:, :, None] * pattern[None, :, :], axis=1)
    hits = jnp.any(listed[:, :, None] == natural_cols[None, None, :], axis=1)
    return hits.astype(jnp.float32)


def fold_product(left, panel):
    return jnp.dot(
        lax.all_gather(left, "row", axis=1, tiled=True),
        panel,
        precision=lax.Precision.HIGHEST,
        preferred_element_type=jnp.float32,
    )


def panels(block, density, pattern, grid_order):
    row_count, col_count = density.shape
    row_blocks = row_count // block
    col_blocks = col_count // block
    first_row = lax.axis_index(("col", "rep")) * row_blocks
    first_col = lax.axis_index("row") * col_blocks
    hits = block_mask(pattern, grid_order, first_row, first_col, row_blocks, col_blocks)
    mask = jnp.broadcast_to(hits[:, None, :, None], (row_blocks, block, col_blocks, block)).reshape(
        row_count, col_count
    )
    current = density
    for repeat in range(STEPS):
        panel = lax.all_gather(current, ("col", "rep"), axis=0, tiled=True)
        square = fold_product(current, panel)
        cube = fold_product(square, panel)
        current = mask * (3.0 * square - 2.0 * cube)
    return current


def split(value):
    high = value.astype(jnp.bfloat16)
    low = (value - high.astype(jnp.float32)).astype(jnp.bfloat16)
    return high, low


def product(ah, al, bh, bl):
    left = jnp.concatenate([ah, ah, al], axis=1)
    right = jnp.concatenate([bh, bl, bh], axis=0)
    return jnp.dot(left, right, preferred_element_type=jnp.float32)


def iotas(side):
    return (
        lax.broadcasted_iota(jnp.int32, (side, side), 0),
        lax.broadcasted_iota(jnp.int32, (side, side), 1),
    )


def chain_groups(rows_n):
    return [group for group in ([0], [*range(1, rows_n - 1)], [rows_n - 1]) if group]


def flipped(group):
    return 1 - group % 2


def place(reps_n):
    rank = lax.axis_index("col") * reps_n + lax.axis_index("rep")
    return rank // 2, rank & 1, lax.axis_index("row")


def pack_kernel(reps_n, x_ref, out_ref):
    side = x_ref.shape[0]
    big_row, core, big_col = place(reps_n)

    @pl.when(big_row != big_col)
    def _():
        pick = jnp.where(big_row < big_col, core, 1 - core)
        out_ref[:side, :] = x_ref[:, pl.ds(pl.multiple_of(pick * side, side), side)]
        out_ref[side:, :] = jnp.zeros((EXTRA, side), jnp.float32)

    @pl.when(big_row == big_col)
    def _():
        i, j = iotas(side)
        own = x_ref[:, pl.ds(pl.multiple_of(core * side, side), side)]
        other = x_ref[:, pl.ds(pl.multiple_of((1 - core) * side, side), side)]
        out_ref[:side, :] = jnp.where(i >= j, own, other)
        diagonal = jnp.sum(jnp.where(i == j, other, 0.0), axis=0, keepdims=True)
        out_ref[side:, :] = jnp.broadcast_to(diagonal, (EXTRA, side))


def write_mask(pattern_ref, order_ref, hits):
    blocks, total = hits.shape
    lane_block = lax.broadcasted_iota(jnp.int32, (1, total), 1) // (total // blocks)
    row_block = lax.broadcasted_iota(jnp.int32, (blocks, 1), 0)
    natural_col = jnp.zeros((1, total), jnp.int32)
    natural_row = jnp.zeros((blocks, 1), jnp.int32)
    for b in range(blocks):
        natural = order_ref[:, b : b + 1]
        natural_col = jnp.where(lane_block == b, natural, natural_col)
        natural_row = jnp.where(row_block == b, natural, natural_row)
    offset = natural_col - natural_row
    offset = jnp.where(offset < 0, offset + blocks, offset)
    hit = jnp.zeros((blocks, total), jnp.bool_)
    for k in range(pattern_ref.shape[1]):
        hit = hit | (offset == pattern_ref[0:1, k : k + 1])
    hits[...] = hit.astype(jnp.float32)


def work_kernel(sizes, *refs):
    rows_n, ranks, reps_n = sizes
    groups = chain_groups(rows_n)
    held, rest = refs[: len(groups)], refs[len(groups) :]
    pattern_ref, order_ref, out_ref, hits, xh, xl, zh, zl, ch, cl = rest
    side = held[0].shape[-1]
    wide = 2 * side
    total = xh.shape[0]
    bigs = total // wide
    blocks = hits.shape[0]
    block = total // blocks
    big_row, core, big_col = place(reps_n)
    links = (ranks // 2).bit_length() - 1

    rank = big_row * 2 + core

    def chunk(a, core_of, b, rows):
        away = rank ^ (a * 2 + core_of)
        swapped = away & 1
        result = None
        for index, group in enumerate(groups):
            order = core ^ swapped ^ flipped(index)
            bits = swapped << links
            for step in range(links):
                bit = jnp.where(order == 0, (away >> (1 + step)) & 1, (away >> (links - step)) & 1)
                bits = bits | (bit << step)
            chain = big_col ^ b
            member = jnp.clip(chain - group[0], 0, len(group) - 1)
            value = held[index][bits * len(group) + member, rows, :]
            result = value if result is None else jnp.where(chain >= group[0], value, result)
        return result

    def put(h, l, value, r, c):
        high, low = split(value)
        h[r, c] = high
        l[r, c] = low

    def span(index, width):
        return slice(index * width, (index + 1) * width)

    def at(index, width):
        return pl.ds(pl.multiple_of(index * width, width), width)

    def unpack(a, b):
        if a != b:
            for j in range(2):
                k = j if a < b else 1 - j
                value = chunk(a, j, b, slice(0, side))
                r, c = span(2 * a + j, side), span(2 * b + k, side)
                put(xh, xl, value, r, c)
                put(xh, xl, value.T, c, r)
            return
        i, j = iotas(side)
        m0 = chunk(a, 0, a, slice(0, side))
        m1 = chunk(a, 1, a, slice(0, side))
        diagonal = chunk(a, 0, a, slice(side, side + 1))
        t0, t1 = m0.T, m1.T
        r0, r1 = span(2 * a, side), span(2 * a + 1, side)
        put(xh, xl, jnp.where(i >= j, m0, t0), r0, r0)
        put(xh, xl, jnp.where(i >= j, m1, t1), r1, r1)
        put(xh, xl, jnp.where(i < j, m0, jnp.where(i > j, t1, diagonal)), r0, r1)
        put(xh, xl, jnp.where(i < j, m1, jnp.where(i > j, t0, diagonal)), r1, r0)

    def masked(value, first_block, cols):
        parts = []
        for b in range(value.shape[0] // block):
            parts.append(value[span(b, block)] * hits[pl.ds(first_block + b, 1), cols])
        return jnp.concatenate(parts, axis=0)

    def mirrored(h, l, value, a, b):
        put(h, l, value, span(a, wide), span(b, wide))
        if a != b:
            put(h, l, value.T, span(b, wide), span(a, wide))

    write_mask(pattern_ref, order_ref, hits)

    for b in reversed(range(bigs)):
        for a in reversed(range(b + 1)):
            r, c = span(a, wide), span(b, wide)
            if b == bigs - 1:
                for k in range(a, -1, -1):
                    unpack(a, k)
                    if a != k:
                        unpack(k, a)
            if a == b:
                both = jnp.dot(
                    xh[r, :],
                    jnp.concatenate([xh[:, c], xl[:, c]], axis=1),
                    preferred_element_type=jnp.float32,
                )
                square = both[:, :wide] + (both[:, wide:] + both[:, wide:].T)
            else:
                square = product(xh[r, :], xl[r, :], xh[:, c], xl[:, c])
            value = 3.0 * (xh[r, c].astype(jnp.float32) + xl[r, c].astype(jnp.float32)) - 2.0 * square
            mirrored(zh, zl, value, a, b)

    cols = at(big_col, wide)
    rows = at(rank, side)

    def term(k):
        r = span(k, wide)
        return product(ch[rows, r], cl[rows, r], ch[r, :], cl[r, :])

    square = None
    for b in reversed(range(bigs)):
        for a in reversed(range(b + 1)):
            r, c = span(a, wide), span(b, wide)
            value = product(xh[r, :], xl[r, :], zh[:, c], zl[:, c])
            if a == 0 and b + 1 < bigs:
                square = term(b + 1) if square is None else square + term(b + 1)
            mirrored(ch, cl, masked(value, a * (wide // block), c), a, b)
    square = square + term(0)
    value = 3.0 * (ch[rows, :].astype(jnp.float32) + cl[rows, :].astype(jnp.float32)) - 2.0 * square
    vh, vl = split(value)
    result = product(vh, vl, ch[:, cols], cl[:, cols])
    out_ref[...] = masked(result, rank * (side // block), cols)


def whole(shape, density, pattern, grid_order):
    rows_n, cols_n, reps_n = (shape[name] for name in AXES)
    ranks = cols_n * reps_n
    side, wide = density.shape
    total = side * ranks

    def swap(value, partner):
        pairs = []
        for z in range(rows_n):
            for rank in range(ranks):
                z2, rank2 = partner(z, rank)
                pairs.append((z * ranks + rank, z2 * ranks + rank2))
        return lax.ppermute(value, AXES, pairs)

    vmem = pl.BlockSpec(memory_space=pltpu.VMEM)
    mine = pl.pallas_call(
        functools.partial(pack_kernel, reps_n),
        out_shape=jax.ShapeDtypeStruct((side + EXTRA, side), jnp.float32),
        in_specs=[vmem],
        out_specs=vmem,
        compiler_params=pltpu.CompilerParams(vmem_limit_bytes=PACK_BYTES),
        name="pack",
    )(density)
    links = (ranks // 2).bit_length() - 1
    came = {0: mine[None]}
    for away in range(1, rows_n):
        came[away] = swap(mine, lambda z, r: (z ^ away, r))[None]
    groups = chain_groups(rows_n)
    value = [jnp.concatenate([came[chain] for chain in group], axis=0) for group in groups]
    for step in range(links):
        for k in reversed(range(len(groups))):
            if step and not k:
                value[k], _ = lax.optimization_barrier((value[k], came[rows_n // 2]))
            bits = (2 << step, 1 << (links - step))
            crossed = swap(value[k], lambda z, r: (z, r ^ bits[r % 2 ^ flipped(k)]))
            value[k] = jnp.concatenate([value[k], crossed], axis=0)
    held = []
    for one in value:
        held.append(jnp.concatenate([one, swap(one, lambda z, r: (z, r ^ 1))], axis=0))

    return pl.pallas_call(
        functools.partial(work_kernel, (rows_n, ranks, reps_n)),
        out_shape=jax.ShapeDtypeStruct((side, wide), jnp.float32),
        in_specs=[vmem] * (len(held) + 2),
        out_specs=vmem,
        scratch_shapes=[pltpu.VMEM((grid_order.shape[0], total), jnp.float32)]
        + [pltpu.VMEM((total, total), jnp.bfloat16)] * 6,
        compiler_params=pltpu.CompilerParams(vmem_limit_bytes=WORK_BYTES),
        name="purify",
    )(*held, pattern, grid_order[None])


def fits(shape, side, wide, total):
    sizes = [shape[name] for name in AXES]
    powers = all(size & (size - 1) == 0 for size in sizes)
    ranks = sizes[1] * sizes[2]
    squares = wide == 2 * side and side % 128 == 0 and sizes[0] * 2 == ranks
    return powers and squares and total * total * 24 <= WORK_BYTES


def solution(mesh):
    in_specs = (P(("col", "rep"), "row"), P(), P())
    out_specs = P(("col", "rep"), "row")
    shape = dict(mesh.shape)

    def local(density, pattern, grid_order):
        side, wide = density.shape
        total = side * shape["col"] * shape["rep"]
        if fits(shape, side, wide, total):
            return whole(shape, density, pattern, grid_order)
        return panels(total // grid_order.shape[0], density, pattern, grid_order)

    return jax.shard_map(local, mesh=mesh, in_specs=in_specs, out_specs=out_specs, check_vma=False)
```

```python
import functools

import jax
import jax.numpy as jnp
from jax import lax
from jax.experimental import pallas as pl
from jax.experimental.pallas import tpu as pltpu
from jax.sharding import PartitionSpec as P

STEPS = 2
AXES = ("row", "col", "rep")
PACK_BYTES = 2 * 2**20
WORK_BYTES = 28 * 2**20
EXTRA = 8


def block_mask(pattern, grid_order, first_row, first_col, row_blocks, col_blocks):
    total = grid_order.shape[0]
    every = jnp.arange(total, dtype=jnp.int32)
    row_ids = first_row + jnp.arange(row_blocks, dtype=jnp.int32)
    col_ids = first_col + jnp.arange(col_blocks, dtype=jnp.int32)
    row_pick = (row_ids[:, None] == every[None, :]).astype(jnp.int32)
    col_pick = (col_ids[:, None] == every[None, :]).astype(jnp.int32)
    natural_rows = jnp.sum(row_pick * grid_order[None, :], axis=1)
    natural_cols = jnp.sum(col_pick * grid_order[None, :], axis=1)
    row_select = (natural_rows[:, None] == every[None, :]).astype(jnp.int32)
    listed = jnp.sum(row_select[:, :, None] * pattern[None, :, :], axis=1)
    hits = jnp.any(listed[:, :, None] == natural_cols[None, None, :], axis=1)
    return hits.astype(jnp.float32)


def fold_product(left, panel):
    return jnp.dot(
        lax.all_gather(left, "row", axis=1, tiled=True),
        panel,
        precision=lax.Precision.HIGHEST,
        preferred_element_type=jnp.float32,
    )


def panels(block, density, pattern, grid_order):
    row_count, col_count = density.shape
    row_blocks = row_count // block
    col_blocks = col_count // block
    first_row = lax.axis_index(("col", "rep")) * row_blocks
    first_col = lax.axis_index("row") * col_blocks
    hits = block_mask(pattern, grid_order, first_row, first_col, row_blocks, col_blocks)
    mask = jnp.broadcast_to(hits[:, None, :, None], (row_blocks, block, col_blocks, block)).reshape(
        row_count, col_count
    )
    current = density
    for repeat in range(STEPS):
        panel = lax.all_gather(current, ("col", "rep"), axis=0, tiled=True)
        square = fold_product(current, panel)
        cube = fold_product(square, panel)
        current = mask * (3.0 * square - 2.0 * cube)
    return current


def split(value):
    high = value.astype(jnp.bfloat16)
    low = (value - high.astype(jnp.float32)).astype(jnp.bfloat16)
    return high, low


def product(ah, al, bh, bl):
    left = jnp.concatenate([ah, ah, al], axis=1)
    right = jnp.concatenate([bh, bl, bh], axis=0)
    return jnp.dot(left, right, preferred_element_type=jnp.float32)


def iotas(side):
    return (
        lax.broadcasted_iota(jnp.int32, (side, side), 0),
        lax.broadcasted_iota(jnp.int32, (side, side), 1),
    )


def chain_groups(rows_n):
    return [group for group in ([0], [*range(1, rows_n - 1)], [rows_n - 1]) if group]


def flipped(group):
    return 1 - group % 2


def form(d, a):
    return (d & 1 & (a ^ a >> 1)) ^ (d >> 1 & a >> 1)


def place(reps_n):
    rank = lax.axis_index("col") * reps_n + lax.axis_index("rep")
    return rank // 2, rank & 1, lax.axis_index("row")


def pack_kernel(reps_n, x_ref, out_ref):
    side = x_ref.shape[0]
    big_row, core, big_col = place(reps_n)

    @pl.when(big_row != big_col)
    def _():
        pick = core ^ form(big_row ^ big_col, big_row)
        out_ref[:side, :] = x_ref[:, pl.ds(pl.multiple_of(pick * side, side), side)]
        out_ref[side:, :] = jnp.zeros((EXTRA, side), jnp.float32)

    @pl.when(big_row == big_col)
    def _():
        i, j = iotas(side)
        own = x_ref[:, pl.ds(pl.multiple_of(core * side, side), side)]
        other = x_ref[:, pl.ds(pl.multiple_of((1 - core) * side, side), side)]
        out_ref[:side, :] = jnp.where(i >= j, own, other)
        diagonal = jnp.sum(jnp.where(i == j, other, 0.0), axis=0, keepdims=True)
        out_ref[side:, :] = jnp.broadcast_to(diagonal, (EXTRA, side))


def write_mask(pattern_ref, order_ref, hits, bigs, base):
    blocks, total = hits.shape
    per = blocks // bigs
    half = per // 2

    def actual(index):
        big, within = index // per, index % per
        return (big ^ base) * per + ((within // half) ^ form(big, base)) * half + within % half

    lane_block = actual(lax.broadcasted_iota(jnp.int32, (1, total), 1) // (total // blocks))
    row_block = actual(lax.broadcasted_iota(jnp.int32, (blocks, 1), 0))
    natural_col = jnp.zeros((1, total), jnp.int32)
    natural_row = jnp.zeros((blocks, 1), jnp.int32)
    for b in range(blocks):
        natural = order_ref[:, b : b + 1]
        natural_col = jnp.where(lane_block == b, natural, natural_col)
        natural_row = jnp.where(row_block == b, natural, natural_row)
    offset = natural_col - natural_row
    offset = jnp.where(offset < 0, offset + blocks, offset)
    hit = jnp.zeros((blocks, total), jnp.bool_)
    for k in range(pattern_ref.shape[1]):
        hit = hit | (offset == pattern_ref[0:1, k : k + 1])
    hits[...] = hit.astype(jnp.float32)


def work_kernel(sizes, *refs):
    rows_n, ranks, reps_n = sizes
    groups = chain_groups(rows_n)
    held, rest = refs[: len(groups)], refs[len(groups) :]
    pattern_ref, order_ref, out_ref, hits, xh, xl, zh, zl, ch, cl = rest
    side = held[0].shape[-1]
    wide = 2 * side
    total = xh.shape[0]
    bigs = total // wide
    blocks = hits.shape[0]
    block = total // blocks
    big_row, core, big_col = place(reps_n)
    links = (ranks // 2).bit_length() - 1

    rank = big_row * 2 + core

    def chunk(a, half, b, rows):
        away = rank ^ ((a ^ big_col) * 2 + (half ^ form(a, big_col)))
        (index, group), = [(index, group) for index, group in enumerate(groups) if b in group]
        swapped = away & 1
        order = core ^ swapped ^ flipped(index)
        bits = swapped << links
        for step in range(links):
            bit = jnp.where(order == 0, (away >> (1 + step)) & 1, (away >> (links - step)) & 1)
            bits = bits | (bit << step)
        return held[index][bits * len(group) + group.index(b), rows, :]

    def put(h, l, value, r, c):
        high, low = split(value)
        h[r, c] = high
        l[r, c] = low

    def span(index, width):
        return slice(index * width, (index + 1) * width)

    def at(index, width):
        return pl.ds(pl.multiple_of(index * width, width), width)

    def unpack(a, b):
        if a != b:
            for j in range(2):
                k = j ^ form(a ^ b, a)
                value = chunk(a, j, b, slice(0, side))
                r, c = span(2 * a + j, side), span(2 * b + k, side)
                high, low = split(value)
                xh[r, c], xl[r, c] = high, low
                xh[c, r], xl[c, r] = high.T, low.T
            return
        i, j = iotas(side)
        m0 = chunk(a, 0, a, slice(0, side))
        m1 = chunk(a, 1, a, slice(0, side))
        diagonal = chunk(a, 0, a, slice(side, side + 1))
        t0, t1 = m0.T, m1.T
        r0, r1 = span(2 * a, side), span(2 * a + 1, side)
        put(xh, xl, jnp.where(i >= j, m0, t0), r0, r0)
        put(xh, xl, jnp.where(i >= j, m1, t1), r1, r1)
        put(xh, xl, jnp.where(i < j, m0, jnp.where(i > j, t1, diagonal)), r0, r1)
        put(xh, xl, jnp.where(i < j, m1, jnp.where(i > j, t0, diagonal)), r1, r0)

    def masked(value, first_block, cols):
        parts = []
        for b in range(value.shape[0] // block):
            parts.append(value[span(b, block)] * hits[pl.ds(first_block + b, 1), cols])
        return jnp.concatenate(parts, axis=0)

    def mirrored(h, l, value, a, b):
        high, low = split(value)
        r, c = span(a, wide), span(b, wide)
        h[r, c], l[r, c] = high, low
        if a != b:
            h[c, r], l[c, r] = high.T, low.T

    write_mask(pattern_ref, order_ref, hits, bigs, big_col)

    for b in reversed(range(bigs)):
        for a in reversed(range(b + 1)):
            r, c = span(a, wide), span(b, wide)
            if b == bigs - 1:
                for k in range(a, -1, -1):
                    unpack(a, k)
                    if a != k:
                        unpack(k, a)
            if a == b:
                both = jnp.dot(
                    xh[r, :],
                    jnp.concatenate([xh[:, c], xl[:, c]], axis=1),
                    preferred_element_type=jnp.float32,
                )
                square = both[:, :wide] + (both[:, wide:] + both[:, wide:].T)
            else:
                square = product(xh[r, :], xl[r, :], xh[:, c], xl[:, c])
            value = 3.0 * (xh[r, c].astype(jnp.float32) + xl[r, c].astype(jnp.float32)) - 2.0 * square
            mirrored(zh, zl, value, a, b)

    cols = span(0, wide)
    own = big_row ^ big_col
    own_rank = own * 2 + (core ^ form(own, big_col))
    rows = at(own_rank, side)

    def term(k):
        r = span(k, wide)
        return product(ch[rows, r], cl[rows, r], ch[r, :], cl[r, :])

    square = None
    for b in reversed(range(bigs)):
        for a in reversed(range(b + 1)):
            r, c = span(a, wide), span(b, wide)
            value = product(xh[r, :], xl[r, :], zh[:, c], zl[:, c])
            if a == 0 and b + 1 < bigs:
                square = term(b + 1) if square is None else square + term(b + 1)
            mirrored(ch, cl, masked(value, a * (wide // block), c), a, b)
    square = square + term(0)
    value = 3.0 * (ch[rows, :].astype(jnp.float32) + cl[rows, :].astype(jnp.float32)) - 2.0 * square
    vh, vl = split(value)
    result = product(vh, vl, ch[:, cols], cl[:, cols])
    out_ref[...] = masked(result, own_rank * (side // block), cols)


def whole(shape, density, pattern, grid_order):
    rows_n, cols_n, reps_n = (shape[name] for name in AXES)
    ranks = cols_n * reps_n
    side, wide = density.shape
    total = side * ranks

    def swap(value, partner):
        pairs = []
        for z in range(rows_n):
            for rank in range(ranks):
                z2, rank2 = partner(z, rank)
                pairs.append((z * ranks + rank, z2 * ranks + rank2))
        return lax.ppermute(value, AXES, pairs)

    vmem = pl.BlockSpec(memory_space=pltpu.VMEM)
    mine = pl.pallas_call(
        functools.partial(pack_kernel, reps_n),
        out_shape=jax.ShapeDtypeStruct((side + EXTRA, side), jnp.float32),
        in_specs=[vmem],
        out_specs=vmem,
        compiler_params=pltpu.CompilerParams(vmem_limit_bytes=PACK_BYTES),
        name="pack",
    )(density)
    links = (ranks // 2).bit_length() - 1
    came = {0: mine[None]}
    for away in range(1, rows_n):
        came[away] = swap(mine, lambda z, r: (z ^ away, r))[None]
    groups = chain_groups(rows_n)
    value = [jnp.concatenate([came[chain] for chain in group], axis=0) for group in groups]
    for step in range(links):
        for k in reversed(range(len(groups))):
            if step and not k:
                value[k], _ = lax.optimization_barrier((value[k], came[rows_n // 2]))
            bits = (2 << step, 1 << (links - step))
            crossed = swap(value[k], lambda z, r: (z, r ^ bits[r % 2 ^ flipped(k)]))
            value[k] = jnp.concatenate([value[k], crossed], axis=0)
    held = []
    for one in value:
        held.append(jnp.concatenate([one, swap(one, lambda z, r: (z, r ^ 1))], axis=0))

    return pl.pallas_call(
        functools.partial(work_kernel, (rows_n, ranks, reps_n)),
        out_shape=jax.ShapeDtypeStruct((side, wide), jnp.float32),
        in_specs=[vmem] * (len(held) + 2),
        out_specs=vmem,
        scratch_shapes=[pltpu.VMEM((grid_order.shape[0], total), jnp.float32)]
        + [pltpu.VMEM((total, total), jnp.bfloat16)] * 6,
        compiler_params=pltpu.CompilerParams(vmem_limit_bytes=WORK_BYTES),
        name="purify",
    )(*held, pattern, grid_order[None])


def fits(shape, side, wide, total):
    sizes = [shape[name] for name in AXES]
    powers = all(size & (size - 1) == 0 for size in sizes)
    ranks = sizes[1] * sizes[2]
    squares = wide == 2 * side and side % 128 == 0 and sizes[0] * 2 == ranks and sizes[0] <= 4
    return powers and squares and total * total * 24 <= WORK_BYTES


def solution(mesh):
    in_specs = (P(("col", "rep"), "row"), P(), P())
    out_specs = P(("col", "rep"), "row")
    shape = dict(mesh.shape)

    def local(density, pattern, grid_order):
        side, wide = density.shape
        total = side * shape["col"] * shape["rep"]
        if fits(shape, side, wide, total):
            return whole(shape, density, pattern, grid_order)
        return panels(total // grid_order.shape[0], density, pattern, grid_order)

    return jax.shard_map(local, mesh=mesh, in_specs=in_specs, out_specs=out_specs, check_vma=False)
```

```python
import functools

import jax
import jax.numpy as jnp
from jax import lax
from jax.experimental import pallas as pl
from jax.experimental.pallas import tpu as pltpu
from jax.sharding import PartitionSpec as P

STEPS = 2
AXES = ("row", "col", "rep")
PACK_BYTES = 2 * 2**20
WORK_BYTES = 28 * 2**20
EXTRA = 8


def block_mask(pattern, grid_order, first_row, first_col, row_blocks, col_blocks):
    total = grid_order.shape[0]
    every = jnp.arange(total, dtype=jnp.int32)
    row_ids = first_row + jnp.arange(row_blocks, dtype=jnp.int32)
    col_ids = first_col + jnp.arange(col_blocks, dtype=jnp.int32)
    row_pick = (row_ids[:, None] == every[None, :]).astype(jnp.int32)
    col_pick = (col_ids[:, None] == every[None, :]).astype(jnp.int32)
    natural_rows = jnp.sum(row_pick * grid_order[None, :], axis=1)
    natural_cols = jnp.sum(col_pick * grid_order[None, :], axis=1)
    row_select = (natural_rows[:, None] == every[None, :]).astype(jnp.int32)
    listed = jnp.sum(row_select[:, :, None] * pattern[None, :, :], axis=1)
    hits = jnp.any(listed[:, :, None] == natural_cols[None, None, :], axis=1)
    return hits.astype(jnp.float32)


def fold_product(left, panel):
    return jnp.dot(
        lax.all_gather(left, "row", axis=1, tiled=True),
        panel,
        precision=lax.Precision.HIGHEST,
        preferred_element_type=jnp.float32,
    )


def panels(block, density, pattern, grid_order):
    row_count, col_count = density.shape
    row_blocks = row_count // block
    col_blocks = col_count // block
    first_row = lax.axis_index(("col", "rep")) * row_blocks
    first_col = lax.axis_index("row") * col_blocks
    hits = block_mask(pattern, grid_order, first_row, first_col, row_blocks, col_blocks)
    mask = jnp.broadcast_to(hits[:, None, :, None], (row_blocks, block, col_blocks, block)).reshape(
        row_count, col_count
    )
    current = density
    for repeat in range(STEPS):
        panel = lax.all_gather(current, ("col", "rep"), axis=0, tiled=True)
        square = fold_product(current, panel)
        cube = fold_product(square, panel)
        current = mask * (3.0 * square - 2.0 * cube)
    return current


def split(value):
    high = value.astype(jnp.bfloat16)
    low = (value - high.astype(jnp.float32)).astype(jnp.bfloat16)
    return high, low


def product(ah, al, bh, bl):
    left = jnp.concatenate([ah, ah, al], axis=1)
    right = jnp.concatenate([bh, bl, bh], axis=0)
    return jnp.dot(left, right, preferred_element_type=jnp.float32)


def iotas(side):
    return (
        lax.broadcasted_iota(jnp.int32, (side, side), 0),
        lax.broadcasted_iota(jnp.int32, (side, side), 1),
    )


def chain_groups(rows_n):
    return [group for group in ([0], [*range(1, rows_n - 1)], [rows_n - 1]) if group]


def flipped(group):
    return 1 - group % 2


def form(d, a):
    return (d & 1 & (a ^ a >> 1)) ^ (d >> 1 & a >> 1)


def place(reps_n):
    rank = lax.axis_index("col") * reps_n + lax.axis_index("rep")
    return rank // 2, rank & 1, lax.axis_index("row")


def pack_kernel(reps_n, x_ref, out_ref):
    side = x_ref.shape[0]
    big_row, core, big_col = place(reps_n)

    @pl.when(big_row != big_col)
    def _():
        pick = core ^ form(big_row ^ big_col, big_row)
        out_ref[:side, :] = x_ref[:, pl.ds(pl.multiple_of(pick * side, side), side)]
        out_ref[side:, :] = jnp.zeros((EXTRA, side), jnp.float32)

    @pl.when(big_row == big_col)
    def _():
        i, j = iotas(side)
        own = x_ref[:, pl.ds(pl.multiple_of(core * side, side), side)]
        other = x_ref[:, pl.ds(pl.multiple_of((1 - core) * side, side), side)]
        out_ref[:side, :] = jnp.where(i >= j, own, other)
        diagonal = jnp.sum(jnp.where(i == j, other, 0.0), axis=0, keepdims=True)
        out_ref[side:, :] = jnp.broadcast_to(diagonal, (EXTRA, side))


def write_mask(pattern_ref, order_ref, hits, bigs, base):
    blocks, total = hits.shape
    per = blocks // bigs
    half = per // 2

    def actual(index):
        big, within = index // per, index % per
        return (big ^ base) * per + ((within // half) ^ form(big, base)) * half + within % half

    lane_block = actual(lax.broadcasted_iota(jnp.int32, (1, total), 1) // (total // blocks))
    row_block = actual(lax.broadcasted_iota(jnp.int32, (blocks, 1), 0))
    natural_col = jnp.zeros((1, total), jnp.int32)
    natural_row = jnp.zeros((blocks, 1), jnp.int32)
    for b in range(blocks):
        natural = order_ref[:, b : b + 1]
        natural_col = jnp.where(lane_block == b, natural, natural_col)
        natural_row = jnp.where(row_block == b, natural, natural_row)
    offset = natural_col - natural_row
    offset = jnp.where(offset < 0, offset + blocks, offset)
    hit = jnp.zeros((blocks, total), jnp.bool_)
    for k in range(pattern_ref.shape[1]):
        hit = hit | (offset == pattern_ref[0:1, k : k + 1])
    hits[...] = hit.astype(jnp.float32)


def work_kernel(sizes, *refs):
    rows_n, ranks, reps_n = sizes
    groups = chain_groups(rows_n)
    held, rest = refs[: len(groups)], refs[len(groups) :]
    pattern_ref, order_ref, out_ref, hits, xh, xl, zh, zl, ch, cl = rest
    side = held[0].shape[-1]
    wide = 2 * side
    total = xh.shape[0]
    bigs = total // wide
    blocks = hits.shape[0]
    block = total // blocks
    big_row, core, big_col = place(reps_n)
    links = (ranks // 2).bit_length() - 1

    rank = big_row * 2 + core

    def chunk(a, half, b, rows):
        away = rank ^ ((a ^ big_col) * 2 + (half ^ form(a, big_col)))
        (index, group), = [(index, group) for index, group in enumerate(groups) if b in group]
        swapped = away & 1
        order = core ^ swapped ^ flipped(index)
        bits = swapped << links
        for step in range(links):
            bit = jnp.where(order == 0, (away >> (1 + step)) & 1, (away >> (links - step)) & 1)
            bits = bits | (bit << step)
        return held[index][bits * len(group) + group.index(b), rows, :]

    def put(h, l, value, r, c):
        high, low = split(value)
        h[r, c] = high
        l[r, c] = low

    def span(index, width):
        return slice(index * width, (index + 1) * width)

    def at(index, width):
        return pl.ds(pl.multiple_of(index * width, width), width)

    def unpack(a, b):
        if a != b:
            for j in range(2):
                k = j ^ form(a ^ b, a)
                value = chunk(a, j, b, slice(0, side))
                r, c = span(2 * a + j, side), span(2 * b + k, side)
                high, low = split(value)
                xh[r, c], xl[r, c] = high, low
                xh[c, r], xl[c, r] = high.T, low.T
            return
        i, j = iotas(side)
        m0 = chunk(a, 0, a, slice(0, side))
        m1 = chunk(a, 1, a, slice(0, side))
        diagonal = chunk(a, 0, a, slice(side, side + 1))
        t0, t1 = m0.T, m1.T
        r0, r1 = span(2 * a, side), span(2 * a + 1, side)
        put(xh, xl, jnp.where(i >= j, m0, t0), r0, r0)
        put(xh, xl, jnp.where(i >= j, m1, t1), r1, r1)
        put(xh, xl, jnp.where(i < j, m0, jnp.where(i > j, t1, diagonal)), r0, r1)
        put(xh, xl, jnp.where(i < j, m1, jnp.where(i > j, t0, diagonal)), r1, r0)

    def masked(value, first_block, cols):
        parts = []
        for b in range(value.shape[0] // block):
            parts.append(value[span(b, block)] * hits[pl.ds(first_block + b, 1), cols])
        return jnp.concatenate(parts, axis=0)

    def mirrored(h, l, value, a, b):
        high, low = split(value)
        r, c = span(a, wide), span(b, wide)
        h[r, c], l[r, c] = high, low
        if a != b:
            h[c, r], l[c, r] = high.T, low.T

    for b in reversed(range(bigs)):
        for a in reversed(range(b + 1)):
            r, c = span(a, wide), span(b, wide)
            if b == bigs - 1:
                for k in range(a, -1, -1):
                    unpack(a, k)
                    if a != k:
                        unpack(k, a)
            if a == b:
                both = jnp.dot(
                    xh[r, :],
                    jnp.concatenate([xh[:, c], xl[:, c]], axis=1),
                    preferred_element_type=jnp.float32,
                )
                square = both[:, :wide] + (both[:, wide:] + both[:, wide:].T)
            else:
                square = product(xh[r, :], xl[r, :], xh[:, c], xl[:, c])
            value = 3.0 * (xh[r, c].astype(jnp.float32) + xl[r, c].astype(jnp.float32)) - 2.0 * square
            mirrored(zh, zl, value, a, b)

    write_mask(pattern_ref, order_ref, hits, bigs, big_col)

    cols = span(0, wide)
    own = big_row ^ big_col
    own_rank = own * 2 + (core ^ form(own, big_col))
    rows = at(own_rank, side)

    def term(k):
        r = span(k, wide)
        return product(ch[rows, r], cl[rows, r], ch[r, :], cl[r, :])

    square = None
    for b in reversed(range(bigs)):
        for a in reversed(range(b + 1)):
            r, c = span(a, wide), span(b, wide)
            value = product(xh[r, :], xl[r, :], zh[:, c], zl[:, c])
            if a == 0 and b + 1 < bigs:
                square = term(b + 1) if square is None else square + term(b + 1)
            mirrored(ch, cl, masked(value, a * (wide // block), c), a, b)
    square = square + term(0)
    value = 3.0 * (ch[rows, :].astype(jnp.float32) + cl[rows, :].astype(jnp.float32)) - 2.0 * square
    vh, vl = split(value)
    result = product(vh, vl, ch[:, cols], cl[:, cols])
    out_ref[...] = masked(result, own_rank * (side // block), cols)


def whole(shape, density, pattern, grid_order):
    rows_n, cols_n, reps_n = (shape[name] for name in AXES)
    ranks = cols_n * reps_n
    side, wide = density.shape
    total = side * ranks

    def swap(value, partner):
        pairs = []
        for z in range(rows_n):
            for rank in range(ranks):
                z2, rank2 = partner(z, rank)
                pairs.append((z * ranks + rank, z2 * ranks + rank2))
        return lax.ppermute(value, AXES, pairs)

    vmem = pl.BlockSpec(memory_space=pltpu.VMEM)
    mine = pl.pallas_call(
        functools.partial(pack_kernel, reps_n),
        out_shape=jax.ShapeDtypeStruct((side + EXTRA, side), jnp.float32),
        in_specs=[vmem],
        out_specs=vmem,
        compiler_params=pltpu.CompilerParams(vmem_limit_bytes=PACK_BYTES),
        name="pack",
    )(density)
    links = (ranks // 2).bit_length() - 1
    came = {0: mine[None]}
    for away in reversed(range(1, rows_n)):
        came[away] = swap(mine, lambda z, r: (z ^ away, r))[None]
    groups = chain_groups(rows_n)
    value = [jnp.concatenate([came[chain] for chain in group], axis=0) for group in groups]
    for step in range(links):
        for k in reversed(range(len(groups))):
            if step and not k:
                value[k], _ = lax.optimization_barrier((value[k], came[rows_n // 2]))
            bits = (2 << step, 1 << (links - step))
            crossed = swap(value[k], lambda z, r: (z, r ^ bits[r % 2 ^ flipped(k)]))
            value[k] = jnp.concatenate([value[k], crossed], axis=0)
    held = []
    for one in value:
        held.append(jnp.concatenate([one, swap(one, lambda z, r: (z, r ^ 1))], axis=0))

    return pl.pallas_call(
        functools.partial(work_kernel, (rows_n, ranks, reps_n)),
        out_shape=jax.ShapeDtypeStruct((side, wide), jnp.float32),
        in_specs=[vmem] * (len(held) + 2),
        out_specs=vmem,
        scratch_shapes=[pltpu.VMEM((grid_order.shape[0], total), jnp.float32)]
        + [pltpu.VMEM((total, total), jnp.bfloat16)] * 6,
        compiler_params=pltpu.CompilerParams(vmem_limit_bytes=WORK_BYTES),
        name="purify",
    )(*held, pattern, grid_order[None])


def fits(shape, side, wide, total):
    sizes = [shape[name] for name in AXES]
    powers = all(size & (size - 1) == 0 for size in sizes)
    ranks = sizes[1] * sizes[2]
    squares = wide == 2 * side and side % 128 == 0 and sizes[0] * 2 == ranks and sizes[0] <= 4
    return powers and squares and total * total * 24 <= WORK_BYTES


def solution(mesh):
    in_specs = (P(("col", "rep"), "row"), P(), P())
    out_specs = P(("col", "rep"), "row")
    shape = dict(mesh.shape)

    def local(density, pattern, grid_order):
        side, wide = density.shape
        total = side * shape["col"] * shape["rep"]
        if fits(shape, side, wide, total):
            return whole(shape, density, pattern, grid_order)
        return panels(total // grid_order.shape[0], density, pattern, grid_order)

    return jax.shard_map(local, mesh=mesh, in_specs=in_specs, out_specs=out_specs, check_vma=False)
```
